256 devices in a mesh: rows: 64 (over x_hi, y, z), cols: 4 (over x_lo, core).
Axes of the slice: x: 4 (x_hi: 2, x_lo: 2; x = x_hi * 2 + x_lo), y: 4, z: 8, core: 2. Of those that a mesh axis runs over, the one named last changes fastest.
Arguments:
- features: float32 [32768, 512], P('rows', 'cols'), may hold values from -6 to 6
- weight_one: float32 [512, 512], P(None, 'cols'), may hold values from -0.25 to 0.25
- weight_two: float32 [512, 512], P(None, 'cols'), may hold values from -0.25 to 0.25
- head_col: float32 [2, 64, 512, 512], P(None, 'rows'), may hold values from -0.125 to 0.125
- diag: float32 [2, 64, 512, 512], P(None, 'rows'), may hold values from -0.125 to 0.125
- head_row: float32 [2, 64, 512, 512], P(None, 'rows'), may hold values from -0.0234375 to 0.0234375
- occupancy: int32 [2, 64, 3], P(None, 'rows'), may hold values 0 or 1
- counts: int32 [2, 64], replicated, may hold values from 1 to 512, 24576 in all within a row
- vertex_lists: int32 [2, 32768], P(None, 'rows'), may hold values from 0 to 32767, as said below
Outputs:
- hidden_two: float32 [32768, 512], P('rows', 'cols')
The draws below stay inside these ranges and needn't reach their ends.
Inputs may be any that keep to these rules, and one draw needn't show every extreme that they name: For each term, vertex_lists[t] is a permutation of 0 to 32767, and the 512 slots of every block row name exactly 8 vertices of every block row.
All inputs are finite; a program needn't handle non-finite values. No bound on the sum of `occupancy` on one device may be relied on, other than what follows from the above.
Results may differ from the reference program's by a relative error of at most 0.0001.
Values sent between devices are 32-bit elements; how exact they have to be, the bound alone decides.
A program may use at most 64 MiB of HBM per device.

```python
import math
import jax
import jax.numpy as jnp
import numpy as np
from jax import lax

F = 512
TILE = 512
TERMS = 2
BLOCKS = 64
VERTS = 32768
GROUP = 8


def draw_vertex_lists(key, part):
    lists = []
    for term in range(TERMS):
        base = jax.random.fold_in(key, 11 + term)
        order_keys = jax.random.split(base, BLOCKS)
        orders = jax.vmap(lambda sub: jax.random.permutation(sub, TILE))(order_keys)
        picks = orders.reshape(BLOCKS, BLOCKS, GROUP) + (jnp.arange(BLOCKS, dtype=jnp.int32) * TILE)[:, None, None]
        picks = jnp.transpose(picks, (1, 0, 2)).reshape(BLOCKS, TILE)
        shuffle_keys = jax.random.split(jax.random.fold_in(base, 7), BLOCKS)
        shuffles = jax.vmap(lambda sub: jax.random.permutation(sub, TILE))(shuffle_keys)
        picks = jnp.take_along_axis(picks, shuffles, axis=1)
        lists.append(picks.reshape(-1))
    return jnp.stack(lists).astype(jnp.int32)


def touch_ends(drawn, own_key, smallest, largest):
    longest = drawn.shape.index(max(drawn.shape))
    spots = []
    for shift in (0, 1):
        where = [jax.random.randint(jax.random.fold_in(own_key, axis), (), 0, length) for axis, length in enumerate(drawn.shape)]
        where[longest] = (where[longest] + shift) % drawn.shape[longest]
        spots.append(tuple(where))
    return drawn.at[spots[0]].set(smallest).at[spots[1]].set(largest)


def block_levels(stream_key, extent, cuts, smallest, top_value):
    def one(dim, blocks):
        heights = jax.random.uniform(jax.random.fold_in(jax.random.fold_in(stream_key, 6), dim), (blocks,), jnp.float32, smallest / len(cuts), top_value / len(cuts))
        return jnp.repeat(jnp.exp(heights), extent[dim] // blocks).reshape((-1,) + (1,) * (len(extent) - dim - 1))

    gain = one(*cuts[0])
    for cut in cuts[1:]:
        gain = gain * one(*cut)
    return gain


def length_profile(amount, total, most, skew):
    weights = [(1 << 20) // math.isqrt(standing ** skew) + 1 for standing in range(2, amount + 1)]
    rest, given = total - most - (amount - 1), [1] * (amount - 1)
    while rest > 0:
        movable = [i for i in range(amount - 1) if given[i] < most]
        mass, remaining = sum([weights[i] for i in movable]), rest
        for i in movable:
            addition = min(most - given[i], max(1, remaining * weights[i] // mass), rest)
            given[i] = given[i] + addition
            rest = rest - addition
    return np.array([most] + given)


def uneven_parts(key, amount, total, most, slope):
    if amount == 2:
        one = jax.random.randint(key, (), max(1, total - most), min(most, total - 1) + 1)
        return jnp.stack([one, total - one])
    tallies = jnp.asarray(length_profile(amount, total, most, slope), jnp.int32)
    couples = (amount - 1) // 2
    giver, receiver = tallies[1:1 + 2 * couples:2], tallies[2:2 + 2 * couples:2]
    room = jnp.minimum(giver - 1, most - receiver)
    passed = jax.random.randint(jax.random.fold_in(key, 1), (couples,), 0, 1 << 20) % (room + 1)
    tallies = tallies.at[1:1 + 2 * couples:2].set(giver - passed).at[2:2 + 2 * couples:2].set(receiver + passed)
    return tallies[jax.random.permutation(jax.random.fold_in(key, 2), amount)]


def noise(rng, extent, spread, most, pieces=(), kind=jnp.bfloat16):
    loudness = block_levels(rng, extent, pieces, -0.22, 0.18) if pieces else 1.0
    entries = jax.random.normal(rng, extent, jnp.float32) * spread * loudness
    return jnp.minimum(jnp.maximum(entries, -most), most).astype(kind)


def setup_inputs(seed: int = 0) -> dict:
    splits = jax.random.split(jax.random.key(seed), 10)
    features = noise(splits[0], (VERTS, F), 1.0, 6.0, ((0, 64), (1, 4)), jnp.float32)
    weight_one = noise(splits[1], (F, F), F ** -0.5, 0.25, ((1, 4),), jnp.float32)
    weight_two = noise(splits[2], (F, F), F ** -0.5, 0.25, ((1, 4),), jnp.float32)
    head_col = noise(splits[3], (TERMS, BLOCKS, TILE, TILE), (4 * TILE) ** -0.5, 0.125, ((1, 64),), jnp.float32)
    diag = noise(splits[4], (TERMS, BLOCKS, TILE, TILE), (4 * TILE) ** -0.5, 0.125, ((1, 64),), jnp.float32)
    head_row = noise(splits[5], (TERMS, BLOCKS, TILE, TILE), (2 * VERTS) ** -0.5, 0.0234375, ((1, 64),), jnp.float32)
    occupancy = touch_ends((jax.random.randint(splits[6], (TERMS, BLOCKS, 3), 0, 4) < 3).astype(jnp.int32), jax.random.fold_in(splits[6], 1), 0, 1)
    counts = jax.vmap(lambda own: uneven_parts(own, BLOCKS, BLOCKS * TILE * 3 // 4, TILE, 2))(jax.random.split(splits[7], TERMS)).reshape((TERMS, BLOCKS)).astype(jnp.int32)
    vertex_lists = draw_vertex_lists(jax.random.fold_in(splits[9], 71), 0)
    return {"features": features, "weight_one": weight_one, "weight_two": weight_two, "head_col": head_col, "diag": diag, "head_row": head_row, "occupancy": occupancy, "counts": counts, "vertex_lists": vertex_lists}


def layer(hidden, weight, head_col, diag, head_row, occupancy, counts, vertex_lists):
    precise = lax.Precision.HIGHEST
    z = jnp.dot(hidden, weight, precision=precise, preferred_element_type=jnp.float32)
    total = jnp.zeros_like(z)
    for term in range(TERMS):
        live = (jnp.arange(TILE, dtype=jnp.int32)[None, :] < counts[term][:, None]).astype(jnp.float32).reshape(-1)
        permuted = (z[vertex_lists[term]] * live[:, None]).reshape(BLOCKS, TILE, -1)
        flags = occupancy[term].astype(jnp.float32)
        result = jnp.einsum("bij,bjf->bif", diag[term], permuted, precision=precise) * flags[:, 0, None, None]
        result = result + jnp.einsum("bij,jf->bif", head_col[term], permuted[0], precision=precise) * flags[:, 1, None, None]
        across = jnp.einsum("bij,bjf->bif", head_row[term], permuted, precision=precise) * flags[:, 2, None, None]
        result = result.at[0].add(jnp.sum(across, axis=0))
        result = result.reshape(VERTS, -1) * live[:, None]
        total = total + jnp.zeros_like(z).at[vertex_lists[term]].set(result)
    return jnp.maximum(total, 0.0)


def reference(features, weight_one, weight_two, head_col, diag, head_row, occupancy, counts, vertex_lists):
    hidden_one = layer(features, weight_one, head_col, diag, head_row, occupancy, counts, vertex_lists)
    return layer(hidden_one, weight_two, head_col, diag, head_row, occupancy, counts, vertex_lists)
```

```python
import jax
import jax.numpy as jnp
from jax import lax
from jax.sharding import PartitionSpec as P


def contract(left, right):
    return jnp.dot(
        left, right, precision=lax.Precision.HIGHEST, preferred_element_type=jnp.float32
    )


def exchange(values):
    return lax.all_to_all(values, "rows", split_axis=0, concat_axis=0, tiled=True)


def shards(
    features, weight_one, weight_two, head_col, diag, head_row, occupancy, counts, vertex_lists
):
    blocks = lax.axis_size("rows")
    myself = lax.axis_index("rows")
    tile = features.shape[0]
    group = tile // blocks
    terms = vertex_lists.shape[0]
    width = features.shape[1]
    slots = jnp.arange(tile, dtype=jnp.int32)
    source = vertex_lists // tile
    local = vertex_lists % tile
    onehot = (source[:, None, :] == jnp.arange(blocks, dtype=jnp.int32)[None, :, None]).astype(
        jnp.float32
    )
    before = (slots[:, None] < slots[None, :]).astype(jnp.float32)
    rank = jnp.sum(jnp.einsum("tbs,sp->tbp", onehot, before) * onehot, axis=1).astype(jnp.int32)
    grouped = source * group + rank
    place = (grouped[:, None, :] == slots[None, :, None]).astype(jnp.float32)
    request = jnp.sum(place * local[:, None, :].astype(jnp.float32), axis=2).astype(jnp.int32)
    message = jnp.transpose(request.reshape(terms, blocks, group), (1, 0, 2))
    first = jnp.broadcast_to(grouped[None], (blocks, terms, tile))
    both = exchange(jnp.concatenate([message.reshape(blocks, -1), first.reshape(blocks, -1)], axis=1))
    asked = both[:, : terms * group].reshape(-1)
    grouped_first = both[0, terms * group :].reshape(terms, tile)
    live = (slots[None, :] < counts[:, myself][:, None]).astype(jnp.float32)
    live_first = (slots[None, :] < counts[:, 0][:, None]).astype(jnp.float32)
    mine = place * live[:, None, :]
    head = (grouped_first[:, None, :] == slots[None, :, None]).astype(jnp.float32)
    head = head * live_first[:, None, :]
    flags = occupancy[:, 0].astype(jnp.float32)

    def fold(rows, tiles, cols, flag):
        return jnp.stack(
            [
                contract(contract(rows[t], tiles[t, 0] * flag[t]), cols[t].T)
                for t in range(terms)
            ]
        )

    diag = fold(mine, diag, mine, flags[:, 0])
    head_col = fold(mine, head_col, head, flags[:, 1])
    head_row = fold(head, head_row, mine, flags[:, 2])
    pick = (asked[:, None] == slots[None, :]).astype(jnp.float32)
    full_one = lax.all_gather(weight_one, "cols", axis=1, tiled=True)

    def spread(values):
        out = contract(pick, values).reshape(blocks, 1, terms, group, width)
        return jnp.concatenate([out, jnp.broadcast_to(out[:1], out.shape)], axis=1)

    def layer(values):
        got = jnp.transpose(exchange(spread(values)), (1, 2, 0, 3, 4)).reshape(2, terms, tile, width)
        own = jnp.stack(
            [contract(diag[t], got[0, t]) + contract(head_col[t], got[1, t]) for t in range(terms)]
        )
        across = jnp.stack([contract(head_row[t], got[0, t]) for t in range(terms)])
        back = jnp.stack([own, across]).reshape(2, terms, blocks, group, width)
        back = exchange(jnp.transpose(back, (2, 0, 1, 3, 4)))
        head_total = jnp.sum(back[:, 1], axis=0)
        rows = back[:, 0].at[0].add(head_total)
        return contract(pick.T, rows.reshape(-1, width))

    wide = lax.all_gather(layer(features), "cols", axis=1, tiled=True)
    hidden = jnp.maximum(contract(wide, full_one), 0.0)
    return jnp.maximum(layer(contract(hidden, weight_two)), 0.0)


def solution(mesh):
    in_specs = (
        P("rows", "cols"),
        P(None, "cols"),
        P(None, "cols"),
        P(None, "rows", None, None),
        P(None, "rows", None, None),
        P(None, "rows", None, None),
        P(None, "rows", None),
        P(),
        P(None, "rows"),
    )
    out_specs = P("rows", "cols")
    return jax.shard_map(shards, mesh=mesh, in_specs=in_specs, out_specs=out_specs, check_vma=False)
```

```python
import jax
import jax.numpy as jnp
from jax import lax
from jax.experimental import pallas as pl
from jax.experimental.pallas import tpu as pltpu
from jax.sharding import PartitionSpec as P

MESH = pl.DeviceIdType.MESH
F32 = jnp.float32
BF16 = jnp.bfloat16
ROWS = 64
COLS = 4
TILE = 512
WIDTH = 128
GROUP = 8
BOTH = 2 * GROUP
CHUNKS = 4
PART = TILE // CHUNKS


def dot(a, b):
    return lax.dot_general(a, b, (((1,), (0,)), ((), ())), preferred_element_type=F32)


def dot_nt(a, b):
    return lax.dot_general(a, b, (((1,), (1,)), ((), ())), preferred_element_type=F32)


def iota(shape, dim):
    return lax.broadcasted_iota(jnp.int32, shape, dim)


def onehot(cond):
    return jnp.where(cond, 1.0, 0.0).astype(BF16)


def halves(value):
    high = value.astype(BF16)
    low = (value - high.astype(F32)).astype(BF16)
    return high, low


def side(value):
    return jnp.concatenate(halves(value), axis=1)


def total(product):
    return product[:, :WIDTH] + product[:, WIDTH:]


def kernel(
    x_ref, w1_ref, w2_ref, hc_ref, dg_ref, hr_ref, occ_ref, cnt_ref, vl_ref,
    o_ref,
    tiles, fold, place, pick, pick_t, idx_out, idx_in, first_out, first_in, w1_all, w1_cat,
    send, arrived, head, back_out, back, part, part_y, sum_y, part_z, sum_z, part_x, wide,
    tile_sem, idx_s, idx_r, first_s, first_r, w_s, w_r, a_s, a_r, h_s, h_r, b_s, b_r, p_s, p_r,
    c_s, c_r,
):
    me = lax.axis_index("rows")
    col = lax.axis_index("cols")
    mx, my, mz = me // 32, (me // 8) % 4, me % 8
    spot = (my * 8 + mz) * 2 + mx

    def remote(src, dst, s, r, row, column):
        return pltpu.make_async_remote_copy(
            src, dst, s, r, device_id=(row, column), device_id_type=MESH
        )

    def peer(j):
        return lax.rem(me + j, ROWS)

    def col_peer(bit):
        core, low = col % 2, col // 2
        if bit & 1:
            core = 1 - core
        if bit & 2:
            low = 1 - low
        return low * 2 + core

    barrier = pltpu.get_barrier_semaphore()

    @pl.loop(1, ROWS)
    def _(j):
        pl.semaphore_signal(barrier, inc=1, device_id=(peer(j), col), device_id_type=MESH)

    for bit in (1, 2, 3):
        pl.semaphore_signal(barrier, inc=1, device_id=(me, col_peer(bit)), device_id_type=MESH)

    loads = []
    for k, ref in enumerate((dg_ref, hc_ref, hr_ref)):
        copy = pltpu.make_async_copy(ref, tiles.at[k], tile_sem.at[k])
        copy.start()
        loads.append(copy)

    upper = onehot(iota((TILE, TILE), 0) < iota((TILE, TILE), 1))
    request = jnp.zeros((ROWS, 128), F32)
    for t in range(2):
        lists = vl_ref[t : t + 1, :]
        source = lists >> 9
        local = lists & 511
        owner = iota((ROWS, TILE), 0) == source
        mask = onehot(owner)
        before = dot(mask, upper)
        rank = jnp.sum(jnp.where(owner, before, 0.0), axis=0, keepdims=True).astype(jnp.int32)
        lane = iota((128, TILE), 0) == rank + t * GROUP
        high = jnp.where(lane, (local >> 1).astype(F32), 0.0).astype(BF16)
        low = jnp.where(lane, (local & 1).astype(F32), 0.0).astype(BF16)
        request = request + 2.0 * dot_nt(mask, high) + dot_nt(mask, low)
        live = iota((1, TILE), 1) < cnt_ref[t, me]
        grouped = source * GROUP + rank
        place[t] = onehot((iota((TILE, TILE), 0) == grouped) & live)
        first_out[t : t + 1, :] = (((source & 31) * 2 + (source >> 5)) * GROUP + rank).astype(F32)
    for b in range(ROWS):
        idx_out[b] = request[b : b + 1, :]

    pl.semaphore_wait(barrier, ROWS - 1 + COLS - 1)

    @pl.loop(1, ROWS)
    def _(j):
        p = peer(j)
        remote(idx_out.at[p], idx_in.at[me], idx_s, idx_r, p, col).start()

    @pl.when(me == 0)
    def _():
        @pl.loop(1, ROWS)
        def _(j):
            remote(first_out, first_in, first_s, first_r, j, col).start()

        first_in[...] = first_out[...]

    idx_in[me] = idx_out[me]
    w1_all[col] = w1_ref[...]
    for bit in (1, 2, 3):
        remote(
            w1_ref, w1_all.at[col], w_s.at[bit - 1], w_r.at[bit - 1], me, col_peer(bit)
        ).start()

    def folded(k, t, rows, cols):
        flag = occ_ref[t, 0, k].astype(F32)
        i = 2 * k + t
        spread = dot(place[rows], side_wide(tiles[k, t] * flag)).astype(BF16)
        both = jnp.concatenate([spread[:, :TILE], spread[:, TILE:]], axis=0)
        fold[i] = dot_nt(both, place[cols]).astype(BF16)

    def side_wide(value):
        return jnp.concatenate(halves(value), axis=1)

    flag_of = {0: 0, 1: 1, 2: 2}
    loads[0].wait()
    for t in range(2):
        folded(flag_of[0], t, t, t)

    pltpu.make_async_copy(
        idx_in.at[pl.ds(0, ROWS - 1)], idx_in.at[pl.ds(0, ROWS - 1)], idx_r
    ).wait()
    asked = jnp.concatenate([idx_in[b] for b in range(ROWS)], axis=0)
    asked_high = (asked.astype(jnp.int32) >> 1).astype(F32)
    asked_low = asked - 2.0 * asked_high
    asked_high, asked_low = asked_high.astype(BF16), asked_low.astype(BF16)
    count = ROWS * BOTH
    repeat = onehot((iota((count, ROWS), 0) >> 4) == iota((count, ROWS), 1))
    keep = (iota((count, 128), 0) & 15) == iota((count, 128), 1)
    ones = jnp.ones((128, TILE), F32).astype(BF16)
    column = 2.0 * dot(
        jnp.where(keep, dot(repeat, asked_high), 0.0).astype(BF16), ones
    ) + dot(jnp.where(keep, dot(repeat, asked_low), 0.0).astype(BF16), ones)
    pick[...] = onehot(column.astype(jnp.int32) == iota((count, TILE), 1))

    def run(layer, rows):
        send[layer] = total(dot(pick[...], side(rows))).reshape(ROWS, BOTH, WIDTH)
        head[layer, spot] = send[layer, 0]
        other = (1 - mx) * 32 + my * 8 + mz
        hx = remote(
            send.at[layer, 0], head.at[layer, spot], h_s.at[layer, 0], h_r.at[layer, 0], other, col
        )
        hx.start()

        @pl.loop(1, ROWS)
        def _(j):
            p = peer(j)
            remote(
                send.at[layer, p], arrived.at[layer, me], a_s.at[layer], a_r.at[layer], p, col
            ).start()

        arrived[layer, me] = send[layer, me]

        if layer == 0:
            lane_of = onehot(iota((128, count), 0) == (iota((128, count), 1) & 15))
            block_of = iota((ROWS, count), 0) == (iota((ROWS, count), 1) >> 4)
            spread = 2.0 * dot(asked_high, lane_of) + dot(asked_low, lane_of)
            line = jnp.sum(jnp.where(block_of, spread, 0.0), axis=0, keepdims=True)
            pick_t[...] = onehot(iota((TILE, count), 0) == line.astype(jnp.int32))

        hx.wait_recv()
        pair = (my * 8 + mz) * 2
        for d in range(1, 8):
            z = (mz + d) % 8
            remote(
                head.at[layer, pl.ds(pair, 2)], head.at[layer, pl.ds(pair, 2)],
                h_s.at[layer, 1], h_r.at[layer, 1], mx * 32 + my * 8 + z, col,
            ).start()

        if layer == 0:
            @pl.when(me != 0)
            def _():
                pltpu.make_async_copy(first_in, first_in, first_r).wait()

            for t in range(2):
                live = iota((1, TILE), 1) < cnt_ref[t, 0]
                line = first_in[t : t + 1, :].astype(jnp.int32)
                place[2 + t] = onehot((iota((TILE, TILE), 0) == line) & live)
            loads[2].wait()
            for t in range(2):
                folded(2, t, 2 + t, t)

        area = head.at[layer, pl.ds(0, 14)]
        pltpu.make_async_copy(area, area, h_r.at[layer, 1]).wait()
        for d in range(1, 4):
            y = (my + d) % 4
            remote(
                head.at[layer, pl.ds(my * 16, 16)], head.at[layer, pl.ds(my * 16, 16)],
                h_s.at[layer, 2], h_r.at[layer, 2], mx * 32 + y * 8 + mz, col,
            ).start()

        if layer == 0:
            loads[1].wait()
            for t in range(2):
                folded(1, t, t, 2 + t)

        area = arrived.at[layer, pl.ds(0, ROWS - 1)]
        pltpu.make_async_copy(area, area, a_r.at[layer]).wait()

        def product(i, right):
            both = dot(fold[i], right)
            return total(both[:TILE] + both[TILE:])

        rights = []
        for t in range(2):
            got = arrived[layer, :, t * GROUP : (t + 1) * GROUP, :].reshape(TILE, WIDTH)
            rights.append(side(got))
            across = product(4 + t, rights[t])
            part[layer, :, t * GROUP : (t + 1) * GROUP, :] = across.reshape(ROWS, GROUP, WIDTH)
        for d in range(1, 4):
            y = (my + d) % 4
            remote(
                part.at[layer, pl.ds(y * 16, 16)], part_y.at[layer, d - 1],
                p_s.at[layer, 0], p_r.at[layer, 0], mx * 32 + y * 8 + mz, col,
            ).start()
        blocks = [product(t, rights[t]) for t in range(2)]

        area = head.at[layer, pl.ds(0, 48)]
        pltpu.make_async_copy(area, area, h_r.at[layer, 2]).wait()
        for t in range(2):
            first = head[layer, :, t * GROUP : (t + 1) * GROUP, :].reshape(TILE, WIDTH)
            block = blocks[t] + product(2 + t, side(first))
            back_out[layer, :, t * GROUP : (t + 1) * GROUP, :] = block.reshape(ROWS, GROUP, WIDTH)

        @pl.loop(1, ROWS)
        def _(j):
            p = peer(j)
            remote(
                back_out.at[layer, p], back.at[layer, me], b_s.at[layer], b_r.at[layer], p, col
            ).start()

        back[layer, me] = back_out[layer, me]

        pltpu.make_async_copy(part_y.at[layer], part_y.at[layer], p_r.at[layer, 0]).wait()
        sum_y[layer] = (
            part[layer, pl.ds(my * 16, 16)]
            + part_y[layer, 0] + part_y[layer, 1] + part_y[layer, 2]
        )
        for d in range(1, 8):
            z = (mz + d) % 8
            remote(
                sum_y.at[layer, pl.ds(z * 2, 2)], part_z.at[layer, d - 1],
                p_s.at[layer, 1], p_r.at[layer, 1], mx * 32 + my * 8 + z, col,
            ).start()
        pltpu.make_async_copy(part_z.at[layer], part_z.at[layer], p_r.at[layer, 1]).wait()
        gathered = sum_y[layer, pl.ds(mz * 2, 2)]
        for d in range(7):
            gathered = gathered + part_z[layer, d]
        sum_z[layer] = gathered
        px = remote(
            sum_z.at[layer, 1 - mx], part_x.at[layer], p_s.at[layer, 2], p_r.at[layer, 2],
            other, col,
        )
        px.start()
        px.wait_recv()
        extra = sum_z[layer, mx] + part_x[layer]

        area = back.at[layer, pl.ds(0, ROWS - 1)]
        pltpu.make_async_copy(area, area, b_r.at[layer]).wait()
        back[layer, 0] = back[layer, 0] + extra
        return total(dot(pick_t[...], side(back[layer].reshape(count, WIDTH))))

    mine = run(0, x_ref[...])

    wide[col] = mine
    near, far, across = col_peer(1), col_peer(2), col_peer(3)
    for k in range(CHUNKS):
        rows = pl.ds(k * PART, PART)
        remote(
            wide.at[col, rows], wide.at[col, rows], c_s.at[0, k], c_r.at[0, k], me, far
        ).start()
    remote(wide.at[col], wide.at[col], c_s.at[1, 0], c_r.at[1, 0], me, near).start()
    for bit in (1, 2, 3):
        remote(
            w1_ref, w1_all.at[col], w_s.at[bit - 1], w_r.at[bit - 1], me, col_peer(bit)
        ).wait()
    for c in range(COLS):
        high, low = halves(w1_all[c])
        w1_cat[:, c * WIDTH : (c + 1) * WIDTH] = high
        w1_cat[:, TILE + c * WIDTH : TILE + (c + 1) * WIDTH] = low
    for k in range(CHUNKS):
        rows = pl.ds(k * PART, PART)
        remote(
            wide.at[col, rows], wide.at[far, rows], c_s.at[0, k], c_r.at[0, k], me, far
        ).wait_recv()
        remote(
            wide.at[far, rows], wide.at[far, rows], c_s.at[2, k], c_r.at[2, k], me, near
        ).start()
    remote(wide.at[col], wide.at[near], c_s.at[1, 0], c_r.at[1, 0], me, near).wait_recv()
    for k in range(CHUNKS):
        rows = pl.ds(k * PART, PART)
        remote(
            wide.at[far, rows], wide.at[across, rows], c_s.at[2, k], c_r.at[2, k], me, near
        ).wait_recv()
    high, low = halves(jnp.concatenate([wide[c] for c in range(COLS)], axis=1))
    both = dot(high, w1_cat[...])
    hidden = both[:, :TILE] + both[:, TILE:] + dot(low, w1_cat[:, :TILE])
    high, low = halves(jnp.maximum(hidden, 0.0))
    w2 = side(w2_ref[...])
    z = total(dot(high, w2)) + dot(low, w2[:, :WIDTH])

    o_ref[...] = jnp.maximum(run(1, z), 0.0)

    def drain(ref, sem):
        pltpu.make_async_copy(ref, ref, sem).wait()

    drain(idx_in.at[pl.ds(0, ROWS - 1)], idx_s)

    @pl.when(me == 0)
    def _():
        @pl.loop(1, ROWS)
        def _(j):
            drain(first_out, first_s)

    for layer in range(2):
        drain(arrived.at[layer, pl.ds(0, ROWS - 1)], a_s.at[layer])
        drain(back.at[layer, pl.ds(0, ROWS - 1)], b_s.at[layer])
        drain(head.at[layer, 0], h_s.at[layer, 0])
        drain(head.at[layer, pl.ds(0, 14)], h_s.at[layer, 1])
        drain(head.at[layer, pl.ds(0, 48)], h_s.at[layer, 2])
        drain(part_y.at[layer], p_s.at[layer, 0])
        drain(part_z.at[layer], p_s.at[layer, 1])
        drain(part_x.at[layer], p_s.at[layer, 2])
    drain(wide.at[0], c_s.at[1, 0])
    for k in range(CHUNKS):
        drain(wide.at[0, pl.ds(0, PART)], c_s.at[0, k])
        drain(wide.at[0, pl.ds(0, PART)], c_s.at[2, k])


def shards(
    features, weight_one, weight_two, head_col, diag, head_row, occupancy, counts, vertex_lists
):
    terms = vertex_lists.shape[0]
    vmem = pl.BlockSpec(memory_space=pltpu.VMEM)
    smem = pl.BlockSpec(memory_space=pltpu.SMEM)
    hbm = pl.BlockSpec(memory_space=pl.ANY)
    count = ROWS * BOTH
    dma = pltpu.SemaphoreType.DMA

    def rows(*lead):
        return pltpu.VMEM(lead + (BOTH, WIDTH), F32)

    return pl.pallas_call(
        kernel,
        out_shape=jax.ShapeDtypeStruct((TILE, WIDTH), F32),
        in_specs=[vmem, vmem, vmem, hbm, hbm, hbm, smem, smem, vmem],
        out_specs=vmem,
        scratch_shapes=[
            pltpu.VMEM((3, terms, TILE, TILE), F32),
            pltpu.VMEM((3 * terms, 2 * TILE, TILE), BF16),
            pltpu.VMEM((2 * terms, TILE, TILE), BF16),
            pltpu.VMEM((count, TILE), BF16),
            pltpu.VMEM((TILE, count), BF16),
            pltpu.VMEM((ROWS, 1, 128), F32),
            pltpu.VMEM((ROWS, 1, 128), F32),
            pltpu.VMEM((terms, TILE), F32),
            pltpu.VMEM((terms, TILE), F32),
            pltpu.VMEM((COLS, TILE, WIDTH), F32),
            pltpu.VMEM((TILE, 2 * TILE), BF16),
            rows(2, ROWS), rows(2, ROWS), rows(2, ROWS), rows(2, ROWS), rows(2, ROWS),
            rows(2, ROWS), rows(2, 3, 16), rows(2, 16), rows(2, 7, 2), rows(2, 2), rows(2),
            pltpu.VMEM((COLS, TILE, WIDTH), F32),
            dma((3,)), dma, dma, dma, dma, dma((3,)), dma((3,)),
            dma((2,)), dma((2,)), dma((2, 3)), dma((2, 3)), dma((2,)), dma((2,)),
            dma((2, 3)), dma((2, 3)), dma((3, CHUNKS)), dma((3, CHUNKS)),
        ],
        compiler_params=pltpu.CompilerParams(
            collective_id=0, has_side_effects=True, vmem_limit_bytes=56 << 20
        ),
    )(
        features, weight_one, weight_two,
        head_col.reshape(terms, TILE, TILE), diag.reshape(terms, TILE, TILE),
        head_row.reshape(terms, TILE, TILE), occupancy, counts, vertex_lists,
    )


def solution(mesh):
    in_specs = (
        P("rows", "cols"),
        P(None, "cols"),
        P(None, "cols"),
        P(None, "rows", None, None),
        P(None, "rows", None, None),
        P(None, "rows", None, None),
        P(None, "rows", None),
        P(),
        P(None, "rows"),
    )
    out_specs = P("rows", "cols")
    return jax.shard_map(shards, mesh=mesh, in_specs=in_specs, out_specs=out_specs, check_vma=False)
```

```python
import jax
import jax.numpy as jnp
from jax import lax
from jax.experimental import pallas as pl
from jax.experimental.pallas import tpu as pltpu
from jax.sharding import PartitionSpec as P

MESH = pl.DeviceIdType.MESH
F32 = jnp.float32
BF16 = jnp.bfloat16
ROWS = 64
COLS = 4
TILE = 512
WIDTH = 128
GROUP = 8
BOTH = 2 * GROUP
CHUNKS = 4
PART = TILE // CHUNKS
HALF = TILE // 2


def dot(a, b):
    return lax.dot_general(a, b, (((1,), (0,)), ((), ())), preferred_element_type=F32)


def dot_nt(a, b):
    return lax.dot_general(a, b, (((1,), (1,)), ((), ())), preferred_element_type=F32)


def iota(shape, dim):
    return lax.broadcasted_iota(jnp.int32, shape, dim)


def onehot(cond):
    return jnp.where(cond, 1.0, 0.0).astype(BF16)


def halves(value):
    high = value.astype(BF16)
    low = (value - high.astype(F32)).astype(BF16)
    return high, low


def side(value):
    return jnp.concatenate(halves(value), axis=1)


def total(product):
    return product[:, :WIDTH] + product[:, WIDTH:]


def kernel(
    x_ref, w1_ref, w2_ref, hc_ref, dg_ref, hr_ref, occ_ref, cnt_ref, vl_ref,
    o_ref,
    tiles, fold, place, pick, pick_t, idx_out, idx_in, first_out, first_in, w1_all, w1_cat,
    send, arrived, first_rows, head, back_out, back, part, part_y, sum_y, part_z, wide,
    tile_sem, idx_s, idx_r, first_s, first_r, w_s, w_r, a_s, a_r, h_s, h_r, b_s, b_r, p_s, p_r,
    c_s, c_r,
):
    me = lax.axis_index("rows")
    col = lax.axis_index("cols")
    mx, my, mz = me // 32, (me // 8) % 4, me % 8
    line_of = me - mz

    def remote(src, dst, s, r, row, column):
        return pltpu.make_async_remote_copy(
            src, dst, s, r, device_id=(row, column), device_id_type=MESH
        )

    def fold_out(i, size):
        return size // 2 + jnp.where(i % 2 == 0, i // 2, -((i + 1) // 2))

    def peer(j):
        x = (mx + 1 - j // 32) % 2
        y = (my + fold_out((j // 8) % 4, 4)) % 4
        z = (mz + fold_out(j % 8, 8)) % 8
        return x * 32 + y * 8 + z

    def along(j):
        return line_of + (mz + fold_out(j, 8)) % 8

    def plane(j):
        return ((mx + 1 - j // 4) % 2) * 32 + ((my + fold_out(j % 4, 4)) % 4) * 8 + mz

    def col_peer(bit):
        core, low = col % 2, col // 2
        if bit & 1:
            core = 1 - core
        if bit & 2:
            low = 1 - low
        return low * 2 + core

    barrier = pltpu.get_barrier_semaphore()

    @pl.loop(0, ROWS - 1)
    def _(j):
        pl.semaphore_signal(barrier, inc=1, device_id=(peer(j), col), device_id_type=MESH)

    for bit in (1, 2, 3):
        pl.semaphore_signal(barrier, inc=1, device_id=(me, col_peer(bit)), device_id_type=MESH)

    loads = []
    for k, ref in enumerate((dg_ref, hc_ref, hr_ref)):
        copy = pltpu.make_async_copy(ref, tiles.at[k], tile_sem.at[k])
        copy.start()
        loads.append(copy)

    upper = onehot(iota((TILE, TILE), 0) < iota((TILE, TILE), 1))
    request = jnp.zeros((ROWS, 128), F32)
    for t in range(2):
        lists = vl_ref[t : t + 1, :]
        source = lists >> 9
        local = lists & 511
        owner = iota((ROWS, TILE), 0) == source
        mask = onehot(owner)
        before = dot(mask, upper)
        rank = jnp.sum(jnp.where(owner, before, 0.0), axis=0, keepdims=True).astype(jnp.int32)
        lane = iota((128, TILE), 0) == rank + t * GROUP
        high = jnp.where(lane, (local >> 1).astype(F32), 0.0).astype(BF16)
        low = jnp.where(lane, (local & 1).astype(F32), 0.0).astype(BF16)
        request = request + 2.0 * dot_nt(mask, high) + dot_nt(mask, low)
        live = iota((1, TILE), 1) < cnt_ref[t, me]
        grouped = source * GROUP + rank
        place[t] = onehot((iota((TILE, TILE), 0) == grouped) & live)
        first_out[t : t + 1, :] = grouped.astype(F32)
    for b in range(ROWS):
        idx_out[b] = request[b : b + 1, :]

    def folded(k, t, rows, cols):
        flag = occ_ref[t, 0, k].astype(F32)
        i = 2 * k + t
        spread = dot(place[rows], side(tiles[k, t] * flag)).astype(BF16)
        both = jnp.concatenate([spread[:, :TILE], spread[:, TILE:]], axis=0)
        fold[i] = dot_nt(both, place[cols]).astype(BF16)

    loads[0].wait()
    for t in range(2):
        folded(0, t, t, t)

    pl.semaphore_wait(barrier, ROWS - 1 + COLS - 1)

    @pl.loop(0, ROWS - 1)
    def _(j):
        p = peer(j)
        remote(idx_out.at[p], idx_in.at[me], idx_s, idx_r, p, col).start()

    @pl.when(me == 0)
    def _():
        @pl.loop(1, ROWS)
        def _(j):
            remote(first_out, first_in, first_s, first_r, j, col).start()

        first_in[...] = first_out[...]

    idx_in[me] = idx_out[me]
    near, far, across = col_peer(1), col_peer(2), col_peer(3)
    w1_all[col] = w1_ref[...]
    remote(w1_ref, w1_all.at[col], w_s.at[1], w_r.at[1], me, far).start()
    remote(w1_ref, w1_all.at[col], w_s.at[0], w_r.at[0], me, near).start()

    pltpu.make_async_copy(
        idx_in.at[pl.ds(0, ROWS - 1)], idx_in.at[pl.ds(0, ROWS - 1)], idx_r
    ).wait()
    asked = jnp.concatenate([idx_in[b] for b in range(ROWS)], axis=0)
    asked_high = (asked.astype(jnp.int32) >> 1).astype(F32)
    asked_low = asked - 2.0 * asked_high
    asked_high, asked_low = asked_high.astype(BF16), asked_low.astype(BF16)
    count = ROWS * BOTH
    repeat = onehot((iota((count, ROWS), 0) >> 4) == iota((count, ROWS), 1))
    keep = (iota((count, 128), 0) & 15) == iota((count, 128), 1)
    ones = jnp.ones((128, TILE), F32).astype(BF16)
    column = 2.0 * dot(
        jnp.where(keep, dot(repeat, asked_high), 0.0).astype(BF16), ones
    ) + dot(jnp.where(keep, dot(repeat, asked_low), 0.0).astype(BF16), ones)
    pick[...] = onehot(column.astype(jnp.int32) == iota((count, TILE), 1))

    def run(layer, rows):
        right = side(rows)
        own = total(dot(pick[0:BOTH, :], right))
        first_rows[layer] = own
        head[layer, me] = own

        @pl.loop(0, 7)
        def _(j):
            remote(
                first_rows.at[layer], head.at[layer, me], h_s.at[layer, 0], h_r.at[layer, 0],
                along(j), col,
            ).start()

        for part_of in range(2):
            half = (mx + 1 - part_of) % 2
            area = pl.ds(pl.multiple_of(half * TILE, TILE), TILE)
            blocks = pl.ds(half * 32, 32)
            send[layer, blocks] = total(dot(pick[area, :], right)).reshape(32, BOTH, WIDTH)

            @pl.loop(part_of * 32, part_of * 31 + 32)
            def _(j):
                p = peer(j)
                remote(
                    send.at[layer, p], arrived.at[layer, me], a_s.at[layer], a_r.at[layer], p, col
                ).start()

        arrived[layer, me] = send[layer, me]

        if layer == 0:
            remote(w1_ref, w1_all.at[far], w_s.at[1], w_r.at[1], me, far).wait_recv()
            remote(w1_all.at[far], w1_all.at[far], w_s.at[2], w_r.at[2], me, near).start()
            lane_of = onehot(iota((128, count), 0) == (iota((128, count), 1) & 15))
            block_of = iota((ROWS, count), 0) == (iota((ROWS, count), 1) >> 4)
            spread = 2.0 * dot(asked_high, lane_of) + dot(asked_low, lane_of)
            line = jnp.sum(jnp.where(block_of, spread, 0.0), axis=0, keepdims=True)
            pick_t[...] = onehot(iota((TILE, count), 0) == line.astype(jnp.int32))

        area = head.at[layer, pl.ds(0, 7)]
        pltpu.make_async_copy(area, area, h_r.at[layer, 0]).wait()

        @pl.loop(0, 7)
        def _(j):
            line = head.at[layer, pl.ds(line_of, 8)]
            remote(line, line, h_s.at[layer, 1], h_r.at[layer, 1], plane(j), col).start()

        if layer == 0:
            @pl.when(me != 0)
            def _():
                pltpu.make_async_copy(first_in, first_in, first_r).wait()

            for t in range(2):
                live = iota((1, TILE), 1) < cnt_ref[t, 0]
                line = first_in[t : t + 1, :].astype(jnp.int32)
                place[2 + t] = onehot((iota((TILE, TILE), 0) == line) & live)
            loads[2].wait()
            for t in range(2):
                folded(2, t, 2 + t, t)
            loads[1].wait()
            for t in range(2):
                folded(1, t, t, 2 + t)

        area = arrived.at[layer, pl.ds(0, ROWS - 1)]
        pltpu.make_async_copy(area, area, a_r.at[layer]).wait()

        def product(i, right):
            both = dot(fold[i], right)
            return total(both[:TILE] + both[TILE:])

        rights = []
        for t in range(2):
            got = arrived[layer, :, t * GROUP : (t + 1) * GROUP, :].reshape(TILE, WIDTH)
            rights.append(side(got))
            across = product(4 + t, rights[t])
            part[layer, :, t * GROUP : (t + 1) * GROUP, :] = across.reshape(ROWS, GROUP, WIDTH)

        @pl.loop(0, 7)
        def _(j):
            p = plane(j)
            remote(
                part.at[layer, pl.ds(p - mz, 8)], part_y.at[layer, j],
                p_s.at[layer, 0], p_r.at[layer, 0], p, col,
            ).start()

        blocks = [product(t, rights[t]) for t in range(2)]

        area = head.at[layer, pl.ds(0, 56)]
        pltpu.make_async_copy(area, area, h_r.at[layer, 1]).wait()
        for t in range(2):
            first = head[layer, :, t * GROUP : (t + 1) * GROUP, :].reshape(TILE, WIDTH)
            block = blocks[t] + product(2 + t, side(first))
            back_out[layer, :, t * GROUP : (t + 1) * GROUP, :] = block.reshape(ROWS, GROUP, WIDTH)

        @pl.loop(0, ROWS - 1)
        def _(j):
            p = peer(j)
            remote(
                back_out.at[layer, p], back.at[layer, me], b_s.at[layer], b_r.at[layer], p, col
            ).start()

        back[layer, me] = back_out[layer, me]

        pltpu.make_async_copy(part_y.at[layer], part_y.at[layer], p_r.at[layer, 0]).wait()
        gathered = part[layer, pl.ds(line_of, 8)]
        for d in range(7):
            gathered = gathered + part_y[layer, d]
        sum_y[layer] = gathered

        @pl.loop(0, 7)
        def _(j):
            p = along(j)
            remote(
                sum_y.at[layer, p % 8], part_z.at[layer, j],
                p_s.at[layer, 1], p_r.at[layer, 1], p, col,
            ).start()

        area = back.at[layer, pl.ds(0, ROWS - 1)]
        pltpu.make_async_copy(area, area, b_r.at[layer]).wait()
        right = side(back[layer].reshape(count, WIDTH))
        sums = [dot(pick_t[k * HALF : (k + 1) * HALF, :], right) for k in range(2)]

        pltpu.make_async_copy(part_z.at[layer], part_z.at[layer], p_r.at[layer, 1]).wait()
        extra = sum_y[layer, mz]
        for d in range(7):
            extra = extra + part_z[layer, d]
        filled = jnp.concatenate([extra, jnp.zeros((WIDTH - BOTH, WIDTH), F32)], axis=0)
        right = side(filled)
        return [
            total(sums[k] + dot(pick_t[k * HALF : (k + 1) * HALF, :WIDTH], right))
            for k in range(2)
        ]

    mine = run(0, x_ref[...])

    def chunk(k):
        return pl.ds(k * PART, PART)

    for k in range(CHUNKS):
        if k % 2 == 0:
            wide[col, pl.ds(k * PART, HALF)] = mine[k // 2]
        remote(
            wide.at[col, chunk(k)], wide.at[col, chunk(k)], c_s.at[0, k], c_r.at[0, k], me, far
        ).start()
    for k in range(CHUNKS):
        remote(
            wide.at[col, chunk(k)], wide.at[col, chunk(k)], c_s.at[1, k], c_r.at[1, k], me, near
        ).start()
    remote(w1_ref, w1_all.at[near], w_s.at[0], w_r.at[0], me, near).wait_recv()
    remote(w1_ref, w1_all.at[across], w_s.at[2], w_r.at[2], me, near).wait_recv()
    for c in range(COLS):
        high, low = halves(w1_all[c])
        w1_cat[:, c * WIDTH : (c + 1) * WIDTH] = high
        w1_cat[:, TILE + c * WIDTH : TILE + (c + 1) * WIDTH] = low
    w2 = side(w2_ref[...])
    mixed = []
    for h in range(2):
        for k in (2 * h, 2 * h + 1):
            remote(
                wide.at[col, chunk(k)], wide.at[far, chunk(k)], c_s.at[0, k], c_r.at[0, k], me, far
            ).wait_recv()
            remote(
                wide.at[far, chunk(k)], wide.at[far, chunk(k)], c_s.at[2, k], c_r.at[2, k], me, near
            ).start()
        for k in (2 * h, 2 * h + 1):
            for step, c in ((1, near), (2, across)):
                remote(
                    wide.at[c, chunk(k)], wide.at[c, chunk(k)], c_s.at[step, k], c_r.at[step, k],
                    me, near,
                ).wait_recv()
        rows = slice(h * HALF, (h + 1) * HALF)
        high, low = halves(jnp.concatenate([wide[c, rows] for c in range(COLS)], axis=1))
        both = dot(high, w1_cat[...])
        hidden = both[:, :TILE] + both[:, TILE:] + dot(low, w1_cat[:, :TILE])
        high, low = halves(jnp.maximum(hidden, 0.0))
        mixed.append(total(dot(high, w2)) + dot(low, w2[:, :WIDTH]))

    for k, value in enumerate(run(1, jnp.concatenate(mixed, axis=0))):
        o_ref[k * HALF : (k + 1) * HALF, :] = jnp.maximum(value, 0.0)

    def drain(ref, sem):
        pltpu.make_async_copy(ref, ref, sem).wait()

    drain(idx_in.at[pl.ds(0, ROWS - 1)], idx_s)

    @pl.when(me == 0)
    def _():
        @pl.loop(1, ROWS)
        def _(j):
            drain(first_out, first_s)

    for layer in range(2):
        drain(arrived.at[layer, pl.ds(0, ROWS - 1)], a_s.at[layer])
        drain(back.at[layer, pl.ds(0, ROWS - 1)], b_s.at[layer])
        drain(head.at[layer, pl.ds(0, 7)], h_s.at[layer, 0])
        drain(head.at[layer, pl.ds(0, 56)], h_s.at[layer, 1])
        drain(part_y.at[layer], p_s.at[layer, 0])
        drain(part_z.at[layer], p_s.at[layer, 1])
    for k in range(3):
        drain(w1_ref, w_s.at[k])
    for k in range(CHUNKS):
        for step in range(3):
            drain(wide.at[0, pl.ds(0, PART)], c_s.at[step, k])


def shards(
    features, weight_one, weight_two, head_col, diag, head_row, occupancy, counts, vertex_lists
):
    terms = vertex_lists.shape[0]
    vmem = pl.BlockSpec(memory_space=pltpu.VMEM)
    smem = pl.BlockSpec(memory_space=pltpu.SMEM)
    hbm = pl.BlockSpec(memory_space=pl.ANY)
    count = ROWS * BOTH
    dma = pltpu.SemaphoreType.DMA

    def rows(*lead):
        return pltpu.VMEM(lead + (BOTH, WIDTH), F32)

    return pl.pallas_call(
        kernel,
        out_shape=jax.ShapeDtypeStruct((TILE, WIDTH), F32),
        in_specs=[vmem, vmem, vmem, hbm, hbm, hbm, smem, smem, vmem],
        out_specs=vmem,
        scratch_shapes=[
            pltpu.VMEM((3, terms, TILE, TILE), F32),
            pltpu.VMEM((3 * terms, 2 * TILE, TILE), BF16),
            pltpu.VMEM((2 * terms, TILE, TILE), BF16),
            pltpu.VMEM((count, TILE), BF16),
            pltpu.VMEM((TILE, count), BF16),
            pltpu.VMEM((ROWS, 1, 128), F32),
            pltpu.VMEM((ROWS, 1, 128), F32),
            pltpu.VMEM((terms, TILE), F32),
            pltpu.VMEM((terms, TILE), F32),
            pltpu.VMEM((COLS, TILE, WIDTH), F32),
            pltpu.VMEM((TILE, 2 * TILE), BF16),
            rows(2, ROWS), rows(2, ROWS), rows(2), rows(2, ROWS), rows(2, ROWS), rows(2, ROWS),
            rows(2, ROWS), rows(2, 7, 8), rows(2, 8), rows(2, 7),
            pltpu.VMEM((COLS, TILE, WIDTH), F32),
            dma((3,)), dma, dma, dma, dma, dma((3,)), dma((3,)),
            dma((2,)), dma((2,)), dma((2, 2)), dma((2, 2)), dma((2,)), dma((2,)),
            dma((2, 2)), dma((2, 2)), dma((3, CHUNKS)), dma((3, CHUNKS)),
        ],
        compiler_params=pltpu.CompilerParams(
            collective_id=0, has_side_effects=True, vmem_limit_bytes=56 << 20
        ),
    )(
        features, weight_one, weight_two,
        head_col.reshape(terms, TILE, TILE), diag.reshape(terms, TILE, TILE),
        head_row.reshape(terms, TILE, TILE), occupancy, counts, vertex_lists,
    )


def solution(mesh):
    in_specs = (
        P("rows", "cols"),
        P(None, "cols"),
        P(None, "cols"),
        P(None, "rows", None, None),
        P(None, "rows", None, None),
        P(None, "rows", None, None),
        P(None, "rows", None),
        P(),
        P(None, "rows"),
    )
    out_specs = P("rows", "cols")
    return jax.shard_map(shards, mesh=mesh, in_specs=in_specs, out_specs=out_specs, check_vma=False)
```

```python
import jax
import jax.numpy as jnp
from jax import lax
from jax.experimental import pallas as pl
from jax.experimental.pallas import tpu as pltpu
from jax.sharding import PartitionSpec as P

MESH = pl.DeviceIdType.MESH
F32 = jnp.float32
BF16 = jnp.bfloat16
ROWS = 64
COLS = 4
TILE = 512
WIDTH = 128
GROUP = 8
BOTH = 2 * GROUP
CHUNKS = 4
PART = TILE // CHUNKS
HALF = TILE // 2


def dot(a, b):
    return lax.dot_general(a, b, (((1,), (0,)), ((), ())), preferred_element_type=F32)


def dot_nt(a, b):
    return lax.dot_general(a, b, (((1,), (1,)), ((), ())), preferred_element_type=F32)


def iota(shape, dim):
    return lax.broadcasted_iota(jnp.int32, shape, dim)


def onehot(cond):
    return jnp.where(cond, 1.0, 0.0).astype(BF16)


def halves(value):
    high = value.astype(BF16)
    low = (value - high.astype(F32)).astype(BF16)
    return high, low


def side(value):
    return jnp.concatenate(halves(value), axis=1)


def total(product):
    return product[:, :WIDTH] + product[:, WIDTH:]


def kernel(
    x_ref, w1_ref, w2_ref, hc_ref, dg_ref, hr_ref, occ_ref, cnt_ref, vl_ref,
    o_ref,
    tiles, fold, place, pick, pick_t, idx_out, idx_in, first_out, first_in, w1_all, w1_cat,
    send, arrived, first_rows, head, back_out, back, part, part_y, sum_y, part_z, wide,
    tile_sem, idx_s, idx_r, first_s, first_r, w_s, w_r, a_s, a_r, h_s, h_r, b_s, b_r, p_s, p_r,
    c_s, c_r,
):
    me = lax.axis_index("rows")
    col = lax.axis_index("cols")
    mx, my, mz = me // 32, (me // 8) % 4, me % 8
    line_of = me - mz

    def remote(src, dst, s, r, row, column):
        return pltpu.make_async_remote_copy(
            src, dst, s, r, device_id=(row, column), device_id_type=MESH
        )

    def fold_out(i, size):
        return size // 2 + jnp.where(i % 2 == 0, i // 2, -((i + 1) // 2))

    def peer(j):
        x = (mx + 1 - j // 32) % 2
        y = (my + fold_out((j // 8) % 4, 4)) % 4
        z = (mz + fold_out(j % 8, 8)) % 8
        return x * 32 + y * 8 + z

    def along(j):
        return line_of + (mz + fold_out(j, 8)) % 8

    def plane(j):
        return ((mx + 1 - j // 4) % 2) * 32 + ((my + fold_out(j % 4, 4)) % 4) * 8 + mz

    def col_peer(bit):
        core, low = col % 2, col // 2
        if bit & 1:
            core = 1 - core
        if bit & 2:
            low = 1 - low
        return low * 2 + core

    barrier = pltpu.get_barrier_semaphore()

    @pl.loop(0, ROWS - 1, unroll=True)
    def _(j):
        pl.semaphore_signal(barrier, inc=1, device_id=(peer(j), col), device_id_type=MESH)

    for bit in (1, 2, 3):
        pl.semaphore_signal(barrier, inc=1, device_id=(me, col_peer(bit)), device_id_type=MESH)

    loads = []
    for k, ref in enumerate((dg_ref, hc_ref, hr_ref)):
        copy = pltpu.make_async_copy(ref, tiles.at[k], tile_sem.at[k])
        copy.start()
        loads.append(copy)

    upper = onehot(iota((TILE, TILE), 0) < iota((TILE, TILE), 1))
    request = jnp.zeros((ROWS, 128), F32)
    for t in range(2):
        lists = vl_ref[t : t + 1, :]
        source = lists >> 9
        local = lists & 511
        owner = iota((ROWS, TILE), 0) == source
        mask = onehot(owner)
        before = dot(mask, upper)
        rank = jnp.sum(jnp.where(owner, before, 0.0), axis=0, keepdims=True).astype(jnp.int32)
        lane = iota((128, TILE), 0) == rank + t * GROUP
        high = jnp.where(lane, (local >> 1).astype(F32), 0.0).astype(BF16)
        low = jnp.where(lane, (local & 1).astype(F32), 0.0).astype(BF16)
        request = request + 2.0 * dot_nt(mask, high) + dot_nt(mask, low)
        live = iota((1, TILE), 1) < cnt_ref[t, me]
        grouped = source * GROUP + rank
        place[t] = onehot((iota((TILE, TILE), 0) == grouped) & live)
        first_out[t : t + 1, :] = grouped.astype(F32)
    for b in range(ROWS):
        idx_out[b] = request[b : b + 1, :]

    def folded(k, t, rows, cols):
        flag = occ_ref[t, 0, k].astype(F32)
        i = 2 * k + t
        spread = dot(place[rows], side(tiles[k, t] * flag)).astype(BF16)
        both = jnp.concatenate([spread[:, :TILE], spread[:, TILE:]], axis=0)
        fold[i] = dot_nt(both, place[cols]).astype(BF16)

    loads[0].wait()
    for t in range(2):
        folded(0, t, t, t)

    pl.semaphore_wait(barrier, ROWS - 1 + COLS - 1)

    @pl.loop(0, ROWS - 1, unroll=True)
    def _(j):
        p = peer(j)
        remote(idx_out.at[p], idx_in.at[me], idx_s, idx_r, p, col).start()

    @pl.when(me == 0)
    def _():
        @pl.loop(1, ROWS)
        def _(j):
            remote(first_out, first_in, first_s, first_r, j, col).start()

        first_in[...] = first_out[...]

    idx_in[me] = idx_out[me]
    near, far, across = col_peer(1), col_peer(2), col_peer(3)
    w1_all[col] = w1_ref[...]
    remote(w1_ref, w1_all.at[col], w_s.at[1], w_r.at[1], me, far).start()
    remote(w1_ref, w1_all.at[col], w_s.at[0], w_r.at[0], me, near).start()

    pltpu.make_async_copy(
        idx_in.at[pl.ds(0, ROWS - 1)], idx_in.at[pl.ds(0, ROWS - 1)], idx_r
    ).wait()
    asked = jnp.concatenate([idx_in[b] for b in range(ROWS)], axis=0)
    asked_high = (asked.astype(jnp.int32) >> 1).astype(F32)
    asked_low = asked - 2.0 * asked_high
    asked_high, asked_low = asked_high.astype(BF16), asked_low.astype(BF16)
    count = ROWS * BOTH
    repeat = onehot((iota((count, ROWS), 0) >> 4) == iota((count, ROWS), 1))
    keep = (iota((count, 128), 0) & 15) == iota((count, 128), 1)
    ones = jnp.ones((128, TILE), F32).astype(BF16)
    column = 2.0 * dot(
        jnp.where(keep, dot(repeat, asked_high), 0.0).astype(BF16), ones
    ) + dot(jnp.where(keep, dot(repeat, asked_low), 0.0).astype(BF16), ones)
    pick[...] = onehot(column.astype(jnp.int32) == iota((count, TILE), 1))

    def run(layer, rows):
        right = side(rows)
        own = total(dot(pick[0:BOTH, :], right))
        first_rows[layer] = own
        head[layer, me] = own

        @pl.loop(0, 7, unroll=True)
        def _(j):
            remote(
                first_rows.at[layer], head.at[layer, me], h_s.at[layer, 0], h_r.at[layer, 0],
                along(j), col,
            ).start()

        for part_of in range(2):
            half = (mx + 1 - part_of) % 2
            area = pl.ds(pl.multiple_of(half * TILE, TILE), TILE)
            blocks = pl.ds(half * 32, 32)
            send[layer, blocks] = total(dot(pick[area, :], right)).reshape(32, BOTH, WIDTH)

            @pl.loop(part_of * 32, part_of * 31 + 32, unroll=True)
            def _(j):
                p = peer(j)
                remote(
                    send.at[layer, p], arrived.at[layer, me], a_s.at[layer], a_r.at[layer], p, col
                ).start()

        arrived[layer, me] = send[layer, me]

        if layer == 0:
            remote(w1_ref, w1_all.at[far], w_s.at[1], w_r.at[1], me, far).wait_recv()
            remote(w1_all.at[far], w1_all.at[far], w_s.at[2], w_r.at[2], me, near).start()
            lane_of = onehot(iota((128, count), 0) == (iota((128, count), 1) & 15))
            block_of = iota((ROWS, count), 0) == (iota((ROWS, count), 1) >> 4)
            spread = 2.0 * dot(asked_high, lane_of) + dot(asked_low, lane_of)
            line = jnp.sum(jnp.where(block_of, spread, 0.0), axis=0, keepdims=True)
            pick_t[...] = onehot(iota((TILE, count), 0) == line.astype(jnp.int32))

        area = head.at[layer, pl.ds(0, 7)]
        pltpu.make_async_copy(area, area, h_r.at[layer, 0]).wait()

        @pl.loop(0, 7, unroll=True)
        def _(j):
            line = head.at[layer, pl.ds(line_of, 8)]
            remote(line, line, h_s.at[layer, 1], h_r.at[layer, 1], plane(j), col).start()

        if layer == 0:
            @pl.when(me != 0)
            def _():
                pltpu.make_async_copy(first_in, first_in, first_r).wait()

            for t in range(2):
                live = iota((1, TILE), 1) < cnt_ref[t, 0]
                line = first_in[t : t + 1, :].astype(jnp.int32)
                place[2 + t] = onehot((iota((TILE, TILE), 0) == line) & live)
            loads[2].wait()
            for t in range(2):
                folded(2, t, 2 + t, t)
            loads[1].wait()
            for t in range(2):
                folded(1, t, t, 2 + t)

        area = arrived.at[layer, pl.ds(0, ROWS - 1)]
        pltpu.make_async_copy(area, area, a_r.at[layer]).wait()

        def product(i, right):
            both = dot(fold[i], right)
            return total(both[:TILE] + both[TILE:])

        rights = []
        for t in range(2):
            got = arrived[layer, :, t * GROUP : (t + 1) * GROUP, :].reshape(TILE, WIDTH)
            rights.append(side(got))
            across = product(4 + t, rights[t])
            part[layer, :, t * GROUP : (t + 1) * GROUP, :] = across.reshape(ROWS, GROUP, WIDTH)

        @pl.loop(0, 7, unroll=True)
        def _(j):
            p = plane(j)
            remote(
                part.at[layer, pl.ds(p - mz, 8)], part_y.at[layer, j],
                p_s.at[layer, 0], p_r.at[layer, 0], p, col,
            ).start()

        blocks = [product(t, rights[t]) for t in range(2)]

        area = head.at[layer, pl.ds(0, 56)]
        pltpu.make_async_copy(area, area, h_r.at[layer, 1]).wait()
        for t in range(2):
            first = head[layer, :, t * GROUP : (t + 1) * GROUP, :].reshape(TILE, WIDTH)
            block = blocks[t] + product(2 + t, side(first))
            back_out[layer, :, t * GROUP : (t + 1) * GROUP, :] = block.reshape(ROWS, GROUP, WIDTH)

        @pl.loop(0, ROWS - 1, unroll=True)
        def _(j):
            p = peer(j)
            remote(
                back_out.at[layer, p], back.at[layer, me], b_s.at[layer], b_r.at[layer], p, col
            ).start()

        back[layer, me] = back_out[layer, me]

        pltpu.make_async_copy(part_y.at[layer], part_y.at[layer], p_r.at[layer, 0]).wait()
        gathered = part[layer, pl.ds(line_of, 8)]
        for d in range(7):
            gathered = gathered + part_y[layer, d]
        sum_y[layer] = gathered

        @pl.loop(0, 7, unroll=True)
        def _(j):
            p = along(j)
            remote(
                sum_y.at[layer, p % 8], part_z.at[layer, j],
                p_s.at[layer, 1], p_r.at[layer, 1], p, col,
            ).start()

        area = back.at[layer, pl.ds(0, ROWS - 1)]
        pltpu.make_async_copy(area, area, b_r.at[layer]).wait()
        right = side(back[layer].reshape(count, WIDTH))
        sums = [dot(pick_t[k * HALF : (k + 1) * HALF, :], right) for k in range(2)]

        pltpu.make_async_copy(part_z.at[layer], part_z.at[layer], p_r.at[layer, 1]).wait()
        extra = sum_y[layer, mz]
        for d in range(7):
            extra = extra + part_z[layer, d]
        filled = jnp.concatenate([extra, jnp.zeros((WIDTH - BOTH, WIDTH), F32)], axis=0)
        right = side(filled)
        return [
            total(sums[k] + dot(pick_t[k * HALF : (k + 1) * HALF, :WIDTH], right))
            for k in range(2)
        ]

    mine = run(0, x_ref[...])

    def chunk(k):
        return pl.ds(k * PART, PART)

    for k in range(CHUNKS):
        if k % 2 == 0:
            wide[col, pl.ds(k * PART, HALF)] = mine[k // 2]
        remote(
            wide.at[col, chunk(k)], wide.at[col, chunk(k)], c_s.at[0, k], c_r.at[0, k], me, far
        ).start()
    for k in range(CHUNKS):
        remote(
            wide.at[col, chunk(k)], wide.at[col, chunk(k)], c_s.at[1, k], c_r.at[1, k], me, near
        ).start()
    remote(w1_ref, w1_all.at[near], w_s.at[0], w_r.at[0], me, near).wait_recv()
    remote(w1_ref, w1_all.at[across], w_s.at[2], w_r.at[2], me, near).wait_recv()
    for c in range(COLS):
        high, low = halves(w1_all[c])
        w1_cat[:, c * WIDTH : (c + 1) * WIDTH] = high
        w1_cat[:, TILE + c * WIDTH : TILE + (c + 1) * WIDTH] = low
    w2 = side(w2_ref[...])
    mixed = []
    for h in range(2):
        for k in (2 * h, 2 * h + 1):
            remote(
                wide.at[col, chunk(k)], wide.at[far, chunk(k)], c_s.at[0, k], c_r.at[0, k], me, far
            ).wait_recv()
            remote(
                wide.at[far, chunk(k)], wide.at[far, chunk(k)], c_s.at[2, k], c_r.at[2, k], me, near
            ).start()
        for k in (2 * h, 2 * h + 1):
            for step, c in ((1, near), (2, across)):
                remote(
                    wide.at[c, chunk(k)], wide.at[c, chunk(k)], c_s.at[step, k], c_r.at[step, k],
                    me, near,
                ).wait_recv()
        rows = slice(h * HALF, (h + 1) * HALF)
        high, low = halves(jnp.concatenate([wide[c, rows] for c in range(COLS)], axis=1))
        both = dot(high, w1_cat[...])
        hidden = both[:, :TILE] + both[:, TILE:] + dot(low, w1_cat[:, :TILE])
        high, low = halves(jnp.maximum(hidden, 0.0))
        mixed.append(total(dot(high, w2)) + dot(low, w2[:, :WIDTH]))

    for k, value in enumerate(run(1, jnp.concatenate(mixed, axis=0))):
        o_ref[k * HALF : (k + 1) * HALF, :] = jnp.maximum(value, 0.0)

    def drain(ref, sem):
        pltpu.make_async_copy(ref, ref, sem).wait()

    drain(idx_in.at[pl.ds(0, ROWS - 1)], idx_s)

    @pl.when(me == 0)
    def _():
        @pl.loop(1, ROWS)
        def _(j):
            drain(first_out, first_s)

    for layer in range(2):
        drain(arrived.at[layer, pl.ds(0, ROWS - 1)], a_s.at[layer])
        drain(back.at[layer, pl.ds(0, ROWS - 1)], b_s.at[layer])
        drain(head.at[layer, pl.ds(0, 7)], h_s.at[layer, 0])
        drain(head.at[layer, pl.ds(0, 56)], h_s.at[layer, 1])
        drain(part_y.at[layer], p_s.at[layer, 0])
        drain(part_z.at[layer], p_s.at[layer, 1])
    for k in range(3):
        drain(w1_ref, w_s.at[k])
    for k in range(CHUNKS):
        for step in range(3):
            drain(wide.at[0, pl.ds(0, PART)], c_s.at[step, k])


def shards(
    features, weight_one, weight_two, head_col, diag, head_row, occupancy, counts, vertex_lists
):
    terms = vertex_lists.shape[0]
    vmem = pl.BlockSpec(memory_space=pltpu.VMEM)
    smem = pl.BlockSpec(memory_space=pltpu.SMEM)
    hbm = pl.BlockSpec(memory_space=pl.ANY)
    count = ROWS * BOTH
    dma = pltpu.SemaphoreType.DMA

    def rows(*lead):
        return pltpu.VMEM(lead + (BOTH, WIDTH), F32)

    return pl.pallas_call(
        kernel,
        out_shape=jax.ShapeDtypeStruct((TILE, WIDTH), F32),
        in_specs=[vmem, vmem, vmem, hbm, hbm, hbm, smem, smem, vmem],
        out_specs=vmem,
        scratch_shapes=[
            pltpu.VMEM((3, terms, TILE, TILE), F32),
            pltpu.VMEM((3 * terms, 2 * TILE, TILE), BF16),
            pltpu.VMEM((2 * terms, TILE, TILE), BF16),
            pltpu.VMEM((count, TILE), BF16),
            pltpu.VMEM((TILE, count), BF16),
            pltpu.VMEM((ROWS, 1, 128), F32),
            pltpu.VMEM((ROWS, 1, 128), F32),
            pltpu.VMEM((terms, TILE), F32),
            pltpu.VMEM((terms, TILE), F32),
            pltpu.VMEM((COLS, TILE, WIDTH), F32),
            pltpu.VMEM((TILE, 2 * TILE), BF16),
            rows(2, ROWS), rows(2, ROWS), rows(2), rows(2, ROWS), rows(2, ROWS), rows(2, ROWS),
            rows(2, ROWS), rows(2, 7, 8), rows(2, 8), rows(2, 7),
            pltpu.VMEM((COLS, TILE, WIDTH), F32),
            dma((3,)), dma, dma, dma, dma, dma((3,)), dma((3,)),
            dma((2,)), dma((2,)), dma((2, 2)), dma((2, 2)), dma((2,)), dma((2,)),
            dma((2, 2)), dma((2, 2)), dma((3, CHUNKS)), dma((3, CHUNKS)),
        ],
        compiler_params=pltpu.CompilerParams(
            collective_id=0, has_side_effects=True, vmem_limit_bytes=56 << 20
        ),
    )(
        features, weight_one, weight_two,
        head_col.reshape(terms, TILE, TILE), diag.reshape(terms, TILE, TILE),
        head_row.reshape(terms, TILE, TILE), occupancy, counts, vertex_lists,
    )


def solution(mesh):
    in_specs = (
        P("rows", "cols"),
        P(None, "cols"),
        P(None, "cols"),
        P(None, "rows", None, None),
        P(None, "rows", None, None),
        P(None, "rows", None, None),
        P(None, "rows", None),
        P(),
        P(None, "rows"),
    )
    out_specs = P("rows", "cols")
    return jax.shard_map(shards, mesh=mesh, in_specs=in_specs, out_specs=out_specs, check_vma=False)
```

```python
import jax
import jax.numpy as jnp
from jax import lax
from jax.experimental import pallas as pl
from jax.experimental.pallas import tpu as pltpu
from jax.sharding import PartitionSpec as P

MESH = pl.DeviceIdType.MESH
F32 = jnp.float32
BF16 = jnp.bfloat16
ROWS = 64
COLS = 4
TILE = 512
WIDTH = 128
GROUP = 8
BOTH = 2 * GROUP
CHUNKS = 4
PART = TILE // CHUNKS
HALF = TILE // 2


def dot(a, b):
    return lax.dot_general(a, b, (((1,), (0,)), ((), ())), preferred_element_type=F32)


def dot_nt(a, b):
    return lax.dot_general(a, b, (((1,), (1,)), ((), ())), preferred_element_type=F32)


def iota(shape, dim):
    return lax.broadcasted_iota(jnp.int32, shape, dim)


def onehot(cond):
    return jnp.where(cond, 1.0, 0.0).astype(BF16)


def halves(value):
    high = value.astype(BF16)
    low = (value - high.astype(F32)).astype(BF16)
    return high, low


def side(value):
    return jnp.concatenate(halves(value), axis=1)


def total(product):
    return product[:, :WIDTH] + product[:, WIDTH:]


def kernel(
    x_ref, w1_ref, w2_ref, hc_ref, dg_ref, hr_ref, occ_ref, cnt_ref, vl_ref,
    o_ref,
    tiles, fold, place, pick, pick_t, idx_out, idx_in, first_out, first_in, w1_all, w1_cat,
    send, arrived, first_rows, head, back_out, back, part, part_y, sum_y, part_z, wide,
    tile_sem, idx_s, idx_r, first_s, first_r, w_s, w_r, a_s, a_r, h_s, h_r, b_s, b_r, p_s, p_r,
    c_s, c_r,
):
    me = lax.axis_index("rows")
    col = lax.axis_index("cols")
    mx, my, mz = me // 32, (me // 8) % 4, me % 8
    line_of = me - mz

    def remote(src, dst, s, r, row, column):
        return pltpu.make_async_remote_copy(
            src, dst, s, r, device_id=(row, column), device_id_type=MESH
        )

    def fold_out(i, size):
        return size // 2 + jnp.where(i % 2 == 0, i // 2, -((i + 1) // 2))

    def peer(j):
        x = (mx + 1 - j // 32) % 2
        y = (my + fold_out((j // 8) % 4, 4)) % 4
        z = (mz + fold_out(j % 8, 8)) % 8
        return x * 32 + y * 8 + z

    def along(j):
        return line_of + (mz + fold_out(j, 8)) % 8

    def plane(j):
        return ((mx + 1 - j // 4) % 2) * 32 + ((my + fold_out(j % 4, 4)) % 4) * 8 + mz

    def col_peer(bit):
        core, low = col % 2, col // 2
        if bit & 1:
            core = 1 - core
        if bit & 2:
            low = 1 - low
        return low * 2 + core

    barrier = pltpu.get_barrier_semaphore()

    @pl.loop(0, ROWS - 1, unroll=True)
    def _(j):
        pl.semaphore_signal(barrier, inc=1, device_id=(peer(j), col), device_id_type=MESH)

    for bit in (1, 2, 3):
        pl.semaphore_signal(barrier, inc=1, device_id=(me, col_peer(bit)), device_id_type=MESH)

    loads = []
    for k, ref in enumerate((dg_ref, hc_ref, hr_ref)):
        copy = pltpu.make_async_copy(ref, tiles.at[k], tile_sem.at[k])
        copy.start()
        loads.append(copy)

    upper = onehot(iota((TILE, TILE), 0) < iota((TILE, TILE), 1))
    request = jnp.zeros((ROWS, 128), F32)
    for t in range(2):
        lists = vl_ref[t : t + 1, :]
        source = lists >> 9
        local = lists & 511
        owner = iota((ROWS, TILE), 0) == source
        mask = onehot(owner)
        before = dot(mask, upper)
        rank = jnp.sum(jnp.where(owner, before, 0.0), axis=0, keepdims=True).astype(jnp.int32)
        lane = iota((128, TILE), 0) == rank + t * GROUP
        high = jnp.where(lane, (local >> 1).astype(F32), 0.0).astype(BF16)
        low = jnp.where(lane, (local & 1).astype(F32), 0.0).astype(BF16)
        request = request + 2.0 * dot_nt(mask, high) + dot_nt(mask, low)
        live = iota((1, TILE), 1) < cnt_ref[t, me]
        grouped = source * GROUP + rank
        place[t] = onehot((iota((TILE, TILE), 0) == grouped) & live)
        first_out[t : t + 1, :] = grouped.astype(F32)
    for b in range(ROWS):
        idx_out[b] = request[b : b + 1, :]

    def folded(k, t, rows, cols):
        flag = occ_ref[t, 0, k].astype(F32)
        i = 2 * k + t
        spread = dot(place[rows], side(tiles[k, t] * flag)).astype(BF16)
        both = jnp.concatenate([spread[:, :TILE], spread[:, TILE:]], axis=0)
        fold[i] = dot_nt(both, place[cols]).astype(BF16)

    loads[0].wait()
    for t in range(2):
        folded(0, t, t, t)

    pl.semaphore_wait(barrier, ROWS - 1 + COLS - 1)

    @pl.loop(0, ROWS - 1, unroll=True)
    def _(j):
        p = peer(j)
        remote(idx_out.at[p], idx_in.at[me], idx_s, idx_r, p, col).start()

    @pl.when(me == 0)
    def _():
        @pl.loop(1, ROWS, unroll=True)
        def _(j):
            remote(first_out, first_in, first_s, first_r, j, col).start()

        first_in[...] = first_out[...]

    idx_in[me] = idx_out[me]
    near, far, across = col_peer(1), col_peer(2), col_peer(3)
    w1_all[col] = w1_ref[...]
    remote(w1_ref, w1_all.at[col], w_s.at[1], w_r.at[1], me, far).start()
    remote(w1_ref, w1_all.at[col], w_s.at[0], w_r.at[0], me, near).start()

    def stacked(value):
        return jnp.concatenate([value[:, :TILE], value[:, TILE:]], axis=0)

    loads[1].wait()
    loads[2].wait()
    for t in range(2):
        flags = [occ_ref[t, 0, k].astype(F32) for k in range(3)]
        fold[2 + t] = stacked(dot(place[t], side(tiles[1, t] * flags[1])).astype(BF16))
        both = jnp.concatenate(halves(tiles[2, t] * flags[2]), axis=0)
        fold[4 + t] = dot_nt(both, place[t]).astype(BF16)

    pltpu.make_async_copy(
        idx_in.at[pl.ds(0, ROWS - 1)], idx_in.at[pl.ds(0, ROWS - 1)], idx_r
    ).wait()
    asked = jnp.concatenate([idx_in[b] for b in range(ROWS)], axis=0)
    asked_high = (asked.astype(jnp.int32) >> 1).astype(F32)
    asked_low = asked - 2.0 * asked_high
    asked_high, asked_low = asked_high.astype(BF16), asked_low.astype(BF16)
    count = ROWS * BOTH
    repeat = onehot((iota((count, ROWS), 0) >> 4) == iota((count, ROWS), 1))
    keep = (iota((count, 128), 0) & 15) == iota((count, 128), 1)
    ones = jnp.ones((128, TILE), F32).astype(BF16)
    column = 2.0 * dot(
        jnp.where(keep, dot(repeat, asked_high), 0.0).astype(BF16), ones
    ) + dot(jnp.where(keep, dot(repeat, asked_low), 0.0).astype(BF16), ones)
    pick[...] = onehot(column.astype(jnp.int32) == iota((count, TILE), 1))

    def run(layer, rows):
        right = side(rows)
        own = total(dot(pick[0:BOTH, :], right))
        first_rows[layer] = own
        head[layer, me] = own

        @pl.loop(0, 7, unroll=True)
        def _(j):
            remote(
                first_rows.at[layer], head.at[layer, me], h_s.at[layer, 0], h_r.at[layer, 0],
                along(j), col,
            ).start()

        for part_of in range(2):
            half = (mx + 1 - part_of) % 2
            area = pl.ds(pl.multiple_of(half * TILE, TILE), TILE)
            blocks = pl.ds(half * 32, 32)
            send[layer, blocks] = total(dot(pick[area, :], right)).reshape(32, BOTH, WIDTH)

            @pl.loop(part_of * 32, part_of * 31 + 32, unroll=True)
            def _(j):
                p = peer(j)
                remote(
                    send.at[layer, p], arrived.at[layer, me], a_s.at[layer], a_r.at[layer], p, col
                ).start()

        arrived[layer, me] = send[layer, me]

        if layer == 0:
            lane_of = onehot(iota((128, count), 0) == (iota((128, count), 1) & 15))
            block_of = iota((ROWS, count), 0) == (iota((ROWS, count), 1) >> 4)
            spread = 2.0 * dot(asked_high, lane_of) + dot(asked_low, lane_of)
            line = jnp.sum(jnp.where(block_of, spread, 0.0), axis=0, keepdims=True)
            pick_t[...] = onehot(iota((TILE, count), 0) == line.astype(jnp.int32))

        area = head.at[layer, pl.ds(0, 7)]
        pltpu.make_async_copy(area, area, h_r.at[layer, 0]).wait()

        @pl.loop(0, 7, unroll=True)
        def _(j):
            line = head.at[layer, pl.ds(line_of, 8)]
            remote(line, line, h_s.at[layer, 1], h_r.at[layer, 1], plane(j), col).start()

        if layer == 0:
            remote(w1_ref, w1_all.at[far], w_s.at[1], w_r.at[1], me, far).wait_recv()
            remote(w1_all.at[far], w1_all.at[far], w_s.at[2], w_r.at[2], me, near).start()
            @pl.when(me != 0)
            def _():
                pltpu.make_async_copy(first_in, first_in, first_r).wait()

            for t in range(2):
                live = iota((1, TILE), 1) < cnt_ref[t, 0]
                line = first_in[t : t + 1, :].astype(jnp.int32)
                place[2 + t] = onehot((iota((TILE, TILE), 0) == line) & live)
            for t in range(2):
                both = jnp.concatenate([fold[4 + t, :TILE, :], fold[4 + t, TILE:, :]], axis=1)
                fold[4 + t] = stacked(dot(place[2 + t], both).astype(BF16))
                fold[2 + t] = dot_nt(fold[2 + t], place[2 + t]).astype(BF16)

        area = arrived.at[layer, pl.ds(0, ROWS - 1)]
        pltpu.make_async_copy(area, area, a_r.at[layer]).wait()

        def product(i, right):
            both = dot(fold[i], right)
            return total(both[:TILE] + both[TILE:])

        rights = []
        for t in range(2):
            got = arrived[layer, :, t * GROUP : (t + 1) * GROUP, :].reshape(TILE, WIDTH)
            rights.append(side(got))
            across = product(4 + t, rights[t])
            part[layer, :, t * GROUP : (t + 1) * GROUP, :] = across.reshape(ROWS, GROUP, WIDTH)

        @pl.loop(0, 7, unroll=True)
        def _(j):
            p = plane(j)
            remote(
                part.at[layer, pl.ds(p - mz, 8)], part_y.at[layer, j],
                p_s.at[layer, 0], p_r.at[layer, 0], p, col,
            ).start()

        blocks = [product(t, rights[t]) for t in range(2)]

        area = head.at[layer, pl.ds(0, 56)]
        pltpu.make_async_copy(area, area, h_r.at[layer, 1]).wait()
        for t in range(2):
            part_t = pl.ds(t * GROUP, GROUP)
            first = head[layer, :, t * GROUP : (t + 1) * GROUP, :].reshape(TILE, WIDTH)
            block = blocks[t] + product(2 + t, side(first))
            back_out[layer, :, t * GROUP : (t + 1) * GROUP, :] = block.reshape(ROWS, GROUP, WIDTH)

            @pl.loop(0, ROWS - 1, unroll=True)
            def _(j):
                p = peer(j)
                remote(
                    back_out.at[layer, p, part_t], back.at[layer, me, part_t],
                    b_s.at[layer], b_r.at[layer], p, col,
                ).start()

        back[layer, me] = back_out[layer, me]

        pltpu.make_async_copy(part_y.at[layer], part_y.at[layer], p_r.at[layer, 0]).wait()
        gathered = part[layer, pl.ds(line_of, 8)]
        for d in range(7):
            gathered = gathered + part_y[layer, d]
        sum_y[layer] = gathered

        @pl.loop(0, 7, unroll=True)
        def _(j):
            p = along(j)
            remote(
                sum_y.at[layer, p % 8], part_z.at[layer, j],
                p_s.at[layer, 1], p_r.at[layer, 1], p, col,
            ).start()

        area = back.at[layer, pl.ds(0, ROWS - 1)]
        pltpu.make_async_copy(area, area, b_r.at[layer]).wait()
        right = side(back[layer].reshape(count, WIDTH))
        sums = [dot(pick_t[k * HALF : (k + 1) * HALF, :], right) for k in range(2)]

        pltpu.make_async_copy(part_z.at[layer], part_z.at[layer], p_r.at[layer, 1]).wait()
        extra = sum_y[layer, mz]
        for d in range(7):
            extra = extra + part_z[layer, d]
        filled = jnp.concatenate([extra, jnp.zeros((WIDTH - BOTH, WIDTH), F32)], axis=0)
        right = side(filled)
        return [
            total(sums[k] + dot(pick_t[k * HALF : (k + 1) * HALF, :WIDTH], right))
            for k in range(2)
        ]

    mine = run(0, x_ref[...])

    def chunk(k):
        return pl.ds(k * PART, PART)

    for k in range(CHUNKS):
        if k % 2 == 0:
            wide[col, pl.ds(k * PART, HALF)] = mine[k // 2]
        remote(
            wide.at[col, chunk(k)], wide.at[col, chunk(k)], c_s.at[0, k], c_r.at[0, k], me, far
        ).start()
    for k in range(CHUNKS):
        remote(
            wide.at[col, chunk(k)], wide.at[col, chunk(k)], c_s.at[1, k], c_r.at[1, k], me, near
        ).start()
    remote(w1_ref, w1_all.at[near], w_s.at[0], w_r.at[0], me, near).wait_recv()
    remote(w1_ref, w1_all.at[across], w_s.at[2], w_r.at[2], me, near).wait_recv()
    for c in range(COLS):
        high, low = halves(w1_all[c])
        w1_cat[:, c * WIDTH : (c + 1) * WIDTH] = high
        w1_cat[:, TILE + c * WIDTH : TILE + (c + 1) * WIDTH] = low
    w2 = side(w2_ref[...])
    mixed = []
    for h in range(2):
        for k in (2 * h, 2 * h + 1):
            remote(
                wide.at[col, chunk(k)], wide.at[far, chunk(k)], c_s.at[0, k], c_r.at[0, k], me, far
            ).wait_recv()
            remote(
                wide.at[far, chunk(k)], wide.at[far, chunk(k)], c_s.at[2, k], c_r.at[2, k], me, near
            ).start()
        for k in (2 * h, 2 * h + 1):
            for step, c in ((1, near), (2, across)):
                remote(
                    wide.at[c, chunk(k)], wide.at[c, chunk(k)], c_s.at[step, k], c_r.at[step, k],
                    me, near,
                ).wait_recv()
        rows = slice(h * HALF, (h + 1) * HALF)
        high, low = halves(jnp.concatenate([wide[c, rows] for c in range(COLS)], axis=1))
        both = dot(high, w1_cat[...])
        hidden = both[:, :TILE] + both[:, TILE:] + dot(low, w1_cat[:, :TILE])
        high, low = halves(jnp.maximum(hidden, 0.0))
        mixed.append(total(dot(high, w2)) + dot(low, w2[:, :WIDTH]))

    for k, value in enumerate(run(1, jnp.concatenate(mixed, axis=0))):
        o_ref[k * HALF : (k + 1) * HALF, :] = jnp.maximum(value, 0.0)

    def drain(ref, sem):
        pltpu.make_async_copy(ref, ref, sem).wait()

    drain(idx_in.at[pl.ds(0, ROWS - 1)], idx_s)

    @pl.when(me == 0)
    def _():
        @pl.loop(1, ROWS)
        def _(j):
            drain(first_out, first_s)

    for layer in range(2):
        drain(arrived.at[layer, pl.ds(0, ROWS - 1)], a_s.at[layer])
        drain(back.at[layer, pl.ds(0, ROWS - 1)], b_s.at[layer])
        drain(head.at[layer, pl.ds(0, 7)], h_s.at[layer, 0])
        drain(head.at[layer, pl.ds(0, 56)], h_s.at[layer, 1])
        drain(part_y.at[layer], p_s.at[layer, 0])
        drain(part_z.at[layer], p_s.at[layer, 1])
    for k in range(3):
        drain(w1_ref, w_s.at[k])
    for k in range(CHUNKS):
        for step in range(3):
            drain(wide.at[0, pl.ds(0, PART)], c_s.at[step, k])


def shards(
    features, weight_one, weight_two, head_col, diag, head_row, occupancy, counts, vertex_lists
):
    terms = vertex_lists.shape[0]
    vmem = pl.BlockSpec(memory_space=pltpu.VMEM)
    smem = pl.BlockSpec(memory_space=pltpu.SMEM)
    hbm = pl.BlockSpec(memory_space=pl.ANY)
    count = ROWS * BOTH
    dma = pltpu.SemaphoreType.DMA

    def rows(*lead):
        return pltpu.VMEM(lead + (BOTH, WIDTH), F32)

    return pl.pallas_call(
        kernel,
        out_shape=jax.ShapeDtypeStruct((TILE, WIDTH), F32),
        in_specs=[vmem, vmem, vmem, hbm, hbm, hbm, smem, smem, vmem],
        out_specs=vmem,
        scratch_shapes=[
            pltpu.VMEM((3, terms, TILE, TILE), F32),
            pltpu.VMEM((3 * terms, 2 * TILE, TILE), BF16),
            pltpu.VMEM((2 * terms, TILE, TILE), BF16),
            pltpu.VMEM((count, TILE), BF16),
            pltpu.VMEM((TILE, count), BF16),
            pltpu.VMEM((ROWS, 1, 128), F32),
            pltpu.VMEM((ROWS, 1, 128), F32),
            pltpu.VMEM((terms, TILE), F32),
            pltpu.VMEM((terms, TILE), F32),
            pltpu.VMEM((COLS, TILE, WIDTH), F32),
            pltpu.VMEM((TILE, 2 * TILE), BF16),
            rows(2, ROWS), rows(2, ROWS), rows(2), rows(2, ROWS), rows(2, ROWS), rows(2, ROWS),
            rows(2, ROWS), rows(2, 7, 8), rows(2, 8), rows(2, 7),
            pltpu.VMEM((COLS, TILE, WIDTH), F32),
            dma((3,)), dma, dma, dma, dma, dma((3,)), dma((3,)),
            dma((2,)), dma((2,)), dma((2, 2)), dma((2, 2)), dma((2,)), dma((2,)),
            dma((2, 2)), dma((2, 2)), dma((3, CHUNKS)), dma((3, CHUNKS)),
        ],
        compiler_params=pltpu.CompilerParams(
            collective_id=0, has_side_effects=True, vmem_limit_bytes=56 << 20
        ),
    )(
        features, weight_one, weight_two,
        head_col.reshape(terms, TILE, TILE), diag.reshape(terms, TILE, TILE),
        head_row.reshape(terms, TILE, TILE), occupancy, counts, vertex_lists,
    )


def solution(mesh):
    in_specs = (
        P("rows", "cols"),
        P(None, "cols"),
        P(None, "cols"),
        P(None, "rows", None, None),
        P(None, "rows", None, None),
        P(None, "rows", None, None),
        P(None, "rows", None),
        P(),
        P(None, "rows"),
    )
    out_specs = P("rows", "cols")
    return jax.shard_map(shards, mesh=mesh, in_specs=in_specs, out_specs=out_specs, check_vma=False)
```
